32 devices in a mesh: ctx: 16 (over z, y, x), head: 2 (over core).
Axes of the slice: x: 2, y: 2, z: 4, core: 2. Of those that a mesh axis runs over, the one named last changes fastest.
Arguments:
- q_self: bfloat16 [2048, 1024], P('ctx', 'head'), may hold values from -6 to 6
- k_self: bfloat16 [2048, 1024], P('ctx', 'head'), may hold values from -6 to 6
- v_self: bfloat16 [2048, 1024], P('ctx', 'head'), may hold values from -6 to 6
- q_cross: bfloat16 [2048, 1024], P('ctx', 'head'), may hold values from -6 to 6
- n_keys: bfloat16 [8192, 1024], P('ctx', 'head'), may hold values from -6 to 6
- n_values: bfloat16 [8192, 1024], P('ctx', 'head'), may hold values from -6 to 6
- d_cross: bfloat16 [2048, 1024], P('ctx', 'head'), may hold values from -16 to 16
Outputs:
- self_out: bfloat16 [2048, 1024], P('ctx', 'head')
- cross_out: bfloat16 [2048, 1024], P('ctx', 'head')
- d_query: bfloat16 [2048, 1024], P('ctx', 'head')
- d_keys: bfloat16 [8192, 1024], P('ctx', 'head')
- d_values: bfloat16 [8192, 1024], P('ctx', 'head')
The draws below stay inside these ranges and needn't reach their ends.
All inputs are finite; a program needn't handle non-finite values.
Results may differ from the reference program's by a relative error of at most 0.012.
Values may be sent and summed in bfloat16 or wider, within the bound.
A program may use at most 128 MiB of HBM per device.

```python
import math
import jax
import jax.numpy as jnp
from jax import lax

HD = 128
SPAN = 64
COLS = 1024
TOKENS = 2048
NROWS = 8192


def base_values(key, offset_tag, row_count):
    folded = jax.random.fold_in(key, offset_tag)
    return jnp.clip(jax.random.normal(folded, (row_count, COLS), jnp.float32), -4.5, 4.5)


def drawn_queries(key, offset_tag, row_count):
    values_drawn = base_values(key, offset_tag, row_count)
    return values_drawn.astype(jnp.bfloat16)


def drawn_keys(key, offset_tag, row_count):
    values_drawn = base_values(key, offset_tag, row_count)
    return values_drawn.astype(jnp.bfloat16)


def draw_q_self(key, part):
    return drawn_queries(key, 100, TOKENS)


def draw_k_self(key, part):
    return drawn_keys(key, 200, TOKENS)


def draw_q_cross(key, part):
    return drawn_queries(key, 300, TOKENS)


def draw_n_keys(key, part):
    return drawn_keys(key, 400, NROWS)


def draw_d_cross(key, part):
    folded = jax.random.fold_in(key, 500)
    position = jnp.arange(TOKENS, dtype=jnp.float32) / TOKENS
    values_drawn = jnp.clip(jax.random.normal(folded, (TOKENS, COLS), jnp.float32), -4.0, 4.0)
    rising = 1.0 + 2.0 * position
    return (values_drawn * rising[:, None]).astype(jnp.bfloat16)


def shard_levels(own_key, extent, split, least, largest):
    loudness, own = 1.0, jax.random.fold_in(own_key, 6)
    for dim, shards_of in split:
        draws = jnp.exp(jax.random.uniform(jax.random.fold_in(own, dim), (shards_of,), jnp.float32, least / len(split), largest / len(split)))
        loudness = loudness * jnp.repeat(draws, extent[dim] // shards_of).reshape([-1 if axis == dim else 1 for axis in range(len(extent))])
    return loudness


def scatter_about(rng, extent, width, reach, pieces=(), kind=jnp.bfloat16):
    drawn = width * jax.random.normal(rng, extent, jnp.float32)
    if pieces:
        drawn = drawn * shard_levels(rng, extent, pieces, -0.22, 0.18)
    return jnp.clip(drawn, -reach, reach).astype(kind)


def setup_inputs(seed: int = 0) -> dict:
    seeds = jax.random.split(jax.random.key(seed), 8)
    return {
        "q_self": draw_q_self(jax.random.fold_in(seeds[7], 71), 0),
        "k_self": draw_k_self(jax.random.fold_in(seeds[7], 71), 0),
        "v_self": scatter_about(seeds[2], (TOKENS, COLS), 1.0, 6.0, ((0, 16), (1, 2))),
        "q_cross": draw_q_cross(jax.random.fold_in(seeds[7], 71), 0),
        "n_keys": draw_n_keys(jax.random.fold_in(seeds[7], 71), 0),
        "n_values": scatter_about(seeds[5], (NROWS, COLS), 1.0, 6.0, ((0, 16), (1, 2))),
        "d_cross": draw_d_cross(jax.random.fold_in(seeds[7], 71), 0),
    }


def causal_block(query_rows, first_position, keys_head, values_head):
    scale_factor = 1.0 / math.sqrt(keys_head.shape[1])
    scores = jnp.dot(query_rows, keys_head.T, preferred_element_type=jnp.float32) * scale_factor
    positions = first_position + jnp.arange(query_rows.shape[0], dtype=jnp.int32)
    key_positions = jnp.arange(keys_head.shape[0], dtype=jnp.int32)
    visible = key_positions[None, :] <= positions[:, None]
    masked = jnp.where(visible, scores, jnp.float32(-1e+30))
    row_max = lax.optimization_barrier(jnp.max(masked, axis=1, keepdims=True))
    weights = jnp.where(visible, jnp.exp(masked - row_max), jnp.float32(0.0))
    row_total = lax.optimization_barrier(jnp.sum(weights, axis=1, keepdims=True))
    mixed = jnp.dot(weights.astype(jnp.bfloat16), values_head, preferred_element_type=jnp.float32)
    return (mixed / row_total).astype(jnp.bfloat16)

def self_attention(q_self, k_self, v_self):
    token_count, column_count = q_self.shape
    head_count = column_count // HD
    block_rows = min(512, token_count)
    block_count = token_count // block_rows

    def by_heads(array):
        return array.reshape(token_count, head_count, HD).transpose(1, 0, 2)

    def per_head(operands):
        query_head, keys_head, values_head = operands
        query_blocks = query_head.reshape(block_count, block_rows, HD)
        firsts = jnp.arange(block_count, dtype=jnp.int32) * block_rows

        def per_block(items):
            return causal_block(items[0], items[1], keys_head, values_head)
        return lax.map(per_block, (query_blocks, firsts)).reshape(token_count, HD)
    result = lax.map(per_head, (by_heads(q_self), by_heads(k_self), by_heads(v_self)))
    return result.transpose(1, 0, 2).reshape(token_count, column_count)

def cross_span(operands):
    query_rows, keys_rows, values_rows, grad_rows = operands
    row_count, column_count = query_rows.shape
    head_count = column_count // HD
    neighbour_count = keys_rows.shape[0]
    scale_factor = 1.0 / math.sqrt(HD)
    queries = query_rows.reshape(row_count, head_count, HD).astype(jnp.float32)
    keys_four = keys_rows.reshape(neighbour_count, head_count, HD).astype(jnp.float32)
    values_four = values_rows.reshape(neighbour_count, head_count, HD).astype(jnp.float32)
    grads_four = grad_rows.reshape(row_count, head_count, HD).astype(jnp.float32)
    scores = jnp.einsum('rhd,khd->hrk', queries, keys_four) * scale_factor
    row_max = lax.optimization_barrier(jnp.max(scores, axis=2, keepdims=True))
    weights = jnp.exp(scores - row_max)
    probs = weights / lax.optimization_barrier(jnp.sum(weights, axis=2, keepdims=True))
    probs_low = probs.astype(jnp.bfloat16)
    attended = jnp.einsum('hrk,khd->rhd', probs_low.astype(jnp.float32), values_four)
    grad_probs = jnp.einsum('rhd,khd->hrk', grads_four, values_four)
    centre = lax.optimization_barrier(jnp.sum(grad_probs * probs, axis=2, keepdims=True))
    grad_scores = (probs * (grad_probs - centre) * scale_factor).astype(jnp.bfloat16)
    grad_query = jnp.einsum('hrk,khd->rhd', grad_scores.astype(jnp.float32), keys_four)
    grad_keys = jnp.einsum('hrk,rhd->khd', grad_scores.astype(jnp.float32), queries)
    grad_values = jnp.einsum('hrk,rhd->khd', probs_low.astype(jnp.float32), grads_four)
    return (attended.reshape(row_count, column_count).astype(jnp.bfloat16), grad_query.reshape(row_count, column_count).astype(jnp.bfloat16), grad_keys.reshape(neighbour_count, column_count), grad_values.reshape(neighbour_count, column_count))

def reference(q_self, k_self, v_self, q_cross, n_keys, n_values, d_cross):
    self_out = self_attention(q_self, k_self, v_self)
    token_count, column_count = q_cross.shape
    lag_rows = SPAN - 1
    shifted = jnp.concatenate([q_cross[lag_rows:], jnp.zeros((lag_rows, column_count), jnp.bfloat16)], axis=0)
    span_count = token_count // SPAN
    neighbour_rows = n_keys.shape[0] // span_count
    results = lax.map(cross_span, (shifted.reshape(span_count, SPAN, column_count), n_keys.reshape(span_count, neighbour_rows, column_count), n_values.reshape(span_count, neighbour_rows, column_count), d_cross.reshape(span_count, SPAN, column_count)))
    cross_out = results[0].reshape(token_count, column_count)
    grad_source = results[1].reshape(token_count, column_count)
    d_query = jnp.concatenate([jnp.zeros((lag_rows, column_count), jnp.bfloat16), grad_source[:token_count - lag_rows]], axis=0)
    grad_keys = results[2]
    grad_values = results[3]
    mean_square = (jnp.sum(grad_keys * grad_keys) + jnp.sum(grad_values * grad_values)) / (2.0 * grad_keys.size)
    factor = lax.rsqrt(mean_square + 1e-06)
    d_keys = (grad_keys * factor).astype(jnp.bfloat16).reshape(n_keys.shape)
    d_values = (grad_values * factor).astype(jnp.bfloat16).reshape(n_values.shape)
    return (self_out, cross_out, d_query, d_keys, d_values)
```

```python
import functools
import math

import jax
import jax.numpy as jnp
from jax import lax
from jax.experimental import pallas as pl
from jax.experimental.pallas import tpu as pltpu
from jax.sharding import PartitionSpec as P

HD = 128
SPAN = 64
LAG = SPAN - 1
TAIL = 16
F32 = jnp.float32
BF16 = jnp.bfloat16
NEG = -1e30


def dot(a, b, dims):
    return lax.dot_general(a, b, (dims, ((), ())), preferred_element_type=F32)


def kernel(
    nctx, nhead, group, total_elements,
    q_self, k_self, v_self, q_cross, n_keys, n_values, d_cross,
    self_out, cross_out, d_query, d_keys, d_values,
    kbuf, vbuf, qbuf, osend, orecv, own_o, own_lse,
    qc, nk, nv, dc, shifted, gsrc, cross, dq, gk, gv, dkb, dvb, so,
    sq1, sq2,
    load_sem, out_sem, kv_s, kv_r, q_s, q_r, o_s, o_r, edge_s, edge_r,
    sq1_s, sq1_r, sq2_s, sq2_r,
):
    groups = nctx // group
    rows, cols = q_self.shape
    heads = cols // HD
    nrows = n_keys.shape[0]
    scale = 1.0 / math.sqrt(HD)
    me = lax.axis_index("ctx")
    my_head = lax.axis_index("head")
    hi, lo = me // group, lax.rem(me, group)
    has_next = me < nctx - 1
    has_prev = me > 0

    def hcols(h):
        return pl.ds(pl.multiple_of(h * HD, HD), HD)

    loads = [
        pltpu.make_async_copy(q_cross, qc.at[pl.ds(0, rows)], load_sem.at[0]),
        pltpu.make_async_copy(n_keys, nk, load_sem.at[1]),
        pltpu.make_async_copy(n_values, nv, load_sem.at[2]),
        pltpu.make_async_copy(d_cross, dc, load_sem.at[3]),
        pltpu.make_async_copy(k_self, kbuf.at[lo], load_sem.at[4]),
        pltpu.make_async_copy(v_self, vbuf.at[lo], load_sem.at[5]),
        pltpu.make_async_copy(q_self, qbuf.at[0], load_sem.at[6]),
    ]
    for copy in loads:
        copy.start()

    barrier = pltpu.get_barrier_semaphore()

    def greet(ctx, head):
        pl.semaphore_signal(
            barrier, inc=1, device_id=(ctx, head), device_id_type=pl.DeviceIdType.MESH
        )

    def plane_peer(dl, dh):
        return hi * group + lax.rem(lo + dl, group), lax.rem(my_head + dh, nhead)

    plane_offsets = [(a, b) for a in range(group) for b in range(nhead) if a or b]
    for dl, dh in plane_offsets:
        greet(*plane_peer(dl, dh))
    for d in range(1, groups):
        greet(lax.rem(hi + d, groups) * group + lo, my_head)
    edge_up = jnp.logical_and(lo == group - 1, has_next)
    edge_down = jnp.logical_and(lo == 0, has_prev)

    @pl.when(edge_up)
    def _():
        greet(me + 1, my_head)

    @pl.when(edge_down)
    def _():
        greet(me - 1, my_head)

    pl.semaphore_wait(
        barrier,
        len(plane_offsets) + groups - 1
        + edge_up.astype(jnp.int32) + edge_down.astype(jnp.int32),
    )

    def remote(src, dst, send, recv, ctx, head=None):
        return pltpu.make_async_remote_copy(
            src_ref=src, dst_ref=dst, send_sem=send, recv_sem=recv,
            device_id=(ctx, my_head if head is None else head),
            device_id_type=pl.DeviceIdType.MESH,
        )

    def edge_query():
        return remote(
            q_cross.at[pl.ds(0, SPAN)], qc.at[pl.ds(rows, SPAN)],
            edge_s.at[0], edge_r.at[0], jnp.maximum(me - 1, 0),
        )

    def edge_grad():
        return remote(
            gsrc.at[pl.ds(rows, SPAN)], gsrc.at[pl.ds(0, SPAN)],
            edge_s.at[1], edge_r.at[1], jnp.minimum(me + 1, nctx - 1),
        )

    @pl.when(has_prev)
    def _():
        edge_query().start()

    def kv_copy(d, h, which, slot):
        src, buf = (k_self, kbuf) if which == 0 else (v_self, vbuf)
        return remote(
            src.at[:, hcols(h)], buf.at[slot, :, hcols(h)],
            kv_s.at[d - 1, h, which], kv_r.at[d - 1, h, which],
            hi * group + lax.rem(lo + d, group),
        )

    def q_copy(d, h):
        return remote(
            q_self.at[:, hcols(h)], qbuf.at[d, :, hcols(h)],
            q_s.at[d - 1, h], q_r.at[d - 1, h],
            jnp.maximum(hi - d, 0) * group + lo,
        )

    def o_copy(d, h):
        return remote(
            osend.at[d - 1, h], orecv.at[d - 1, h],
            o_s.at[d - 1, h], o_r.at[d - 1, h],
            jnp.minimum(hi + d, groups - 1) * group + lo,
        )

    @pl.loop(0, heads)
    def _(h):
        for d in range(1, group):
            kv_copy(d, h, 0, lo).start()
            kv_copy(d, h, 1, lo).start()

        @pl.loop(1, groups)
        def _(d):
            @pl.when(hi >= d)
            def _():
                q_copy(d, h).start()

    for copy in loads[:4]:
        copy.wait()

    @pl.when(has_next)
    def _():
        edge_query().wait_recv()

    @pl.when(jnp.logical_not(has_next))
    def _():
        qc[rows:, :] = jnp.zeros((SPAN, cols), BF16)

    row_id = lax.broadcasted_iota(jnp.int32, (rows, rows + SPAN), 0)
    col_id = lax.broadcasted_iota(jnp.int32, (rows, rows + SPAN), 1)
    pick = jnp.where(col_id == row_id + LAG, 1.0, 0.0).astype(BF16)
    shifted[...] = dot(pick, qc[...], ((1,), (0,))).astype(BF16)

    per_span = nrows // (rows // SPAN)
    neighbour = lax.broadcasted_iota(jnp.int32, (nrows, rows), 0)
    query = lax.broadcasted_iota(jnp.int32, (nrows, rows), 1)
    same_span = (neighbour // per_span) == (query // SPAN)

    def cross_head(h, squares):
        c = hcols(h)
        keys, values = nk[:, c], nv[:, c]
        queries, grads = shifted[:, c], dc[:, c]
        st = dot(keys, queries, ((1,), (1,))) * scale
        st = jnp.where(same_span, st, NEG)
        weights = jnp.exp(st - jnp.max(st, axis=0, keepdims=True))
        probs = weights * (1.0 / jnp.sum(weights, axis=0, keepdims=True))
        low = probs.astype(BF16)
        cross[:, c] = dot(low, values, ((0,), (0,))).astype(BF16)
        grad_probs = dot(values, grads, ((1,), (1,)))
        centre = jnp.sum(grad_probs * probs, axis=0, keepdims=True)
        grad_scores = (probs * (grad_probs - centre) * scale).astype(BF16)
        gsrc[SPAN:, c] = dot(grad_scores, keys, ((0,), (0,))).astype(BF16)
        grad_keys = dot(grad_scores, queries, ((1,), (0,)))
        gk[:, c] = grad_keys
        grad_values = dot(low, grads, ((1,), (0,)))
        gv[:, c] = grad_values
        return squares + jnp.sum(
            grad_keys * grad_keys + grad_values * grad_values, axis=0, keepdims=True
        )

    squares = lax.fori_loop(0, heads, cross_head, jnp.zeros((1, HD), F32))
    sq1[0] = jnp.broadcast_to(squares, (8, HD))

    def sq1_copy(dl, dh):
        slot = dl * nhead + dh
        ctx, head = plane_peer(dl, dh)
        return remote(
            sq1.at[0], sq1.at[slot], sq1_s.at[slot], sq1_r.at[slot], ctx, head
        )

    def sq2_copy(d):
        return remote(
            sq2.at[0], sq2.at[d], sq2_s.at[d], sq2_r.at[d],
            lax.rem(hi + d, groups) * group + lo,
        )

    for dl, dh in plane_offsets:
        sq1_copy(dl, dh).start()

    @pl.when(has_next)
    def _():
        edge_grad().start()

    cross_store = pltpu.make_async_copy(cross, cross_out, out_sem.at[0])
    cross_store.start()

    for copy in loads[4:]:
        copy.wait()

    def attend(st, values):
        largest = jnp.max(st, axis=0, keepdims=True)
        weights = jnp.exp(st - largest)
        total = jnp.sum(weights, axis=0, keepdims=True)
        mixed = dot(values, weights.astype(BF16), ((0,), (0,)))
        return mixed * (1.0 / total), largest + jnp.log(total)

    key_id = lax.broadcasted_iota(jnp.int32, (group * rows, rows), 0)
    query_id = lax.broadcasted_iota(jnp.int32, (group * rows, rows), 1)
    tail_id = lax.broadcasted_iota(jnp.int32, (TAIL, HD), 0)

    @pl.loop(0, heads)
    def _(h):
        c = hcols(h)
        for d in range(1, group):
            slot = lax.rem(lo + group - d, group)
            kv_copy(d, h, 0, slot).wait_recv()
            kv_copy(d, h, 1, slot).wait_recv()

        @pl.loop(1, groups)
        def _(step):
            d = groups - step

            @pl.when(hi + d < groups)
            def _():
                q_copy(d, h).wait_recv()
                keys = kbuf[:, :, c].reshape(group * rows, HD)
                values = vbuf[:, :, c].reshape(group * rows, HD)
                mixed, lse = attend(dot(keys, qbuf[d, :, c], ((1,), (1,))) * scale, values)
                osend[d - 1, h, :HD, :] = mixed.astype(BF16)
                high = lse.astype(BF16).astype(F32)
                rest = lse - high
                middle = rest.astype(BF16).astype(F32)
                tail = jnp.where(tail_id == 0, high, jnp.where(tail_id == 1, middle, rest - middle))
                osend[d - 1, h, HD:, :] = tail.astype(BF16)
                o_copy(d, h).start()

        keys = kbuf[:, :, c].reshape(group * rows, HD)
        values = vbuf[:, :, c].reshape(group * rows, HD)
        st = dot(keys, qbuf[0, :, c], ((1,), (1,))) * scale
        st = jnp.where(key_id <= query_id + lo * rows, st, NEG)
        mixed, lse = attend(st, values)
        own_o[h] = mixed
        own_lse[h] = jnp.broadcast_to(lse, (8, HD))

    for dl, dh in plane_offsets:
        sq1_copy(dl, dh).wait_recv()
    sq2[0] = jnp.sum(sq1[...], axis=0)
    for d in range(1, groups):
        sq2_copy(d).start()

    @pl.when(has_prev)
    def _():
        edge_grad().wait_recv()

    @pl.when(jnp.logical_not(has_prev))
    def _():
        gsrc[:SPAN, :] = jnp.zeros((SPAN, cols), BF16)

    back = jnp.where(col_id == row_id + 1, 1.0, 0.0).astype(BF16)
    dq[...] = dot(back, gsrc[...], ((1,), (0,))).astype(BF16)
    query_store = pltpu.make_async_copy(dq, d_query, out_sem.at[1])
    query_store.start()

    for d in range(1, groups):
        sq2_copy(d).wait_recv()
    overall = jnp.sum(jnp.sum(sq2[...], axis=0)[0:1, :], axis=1, keepdims=True)
    factor = lax.rsqrt(overall / total_elements + 1e-06)
    dkb[...] = (gk[...] * factor).astype(BF16)
    keys_store = pltpu.make_async_copy(dkb, d_keys, out_sem.at[2])
    keys_store.start()
    dvb[...] = (gv[...] * factor).astype(BF16)
    values_store = pltpu.make_async_copy(dvb, d_values, out_sem.at[3])
    values_store.start()

    @pl.loop(0, heads)
    def _(h):
        def part(d, state):
            return state

        own_lse[h, 1:2, :] = jnp.ones((1, HD), F32)

        @pl.loop(1, groups)
        def _(d):
            @pl.when(hi >= d)
            def _():
                o_copy(d, h).wait_recv()
                tail = orecv[d - 1, h, HD:, :].astype(F32)
                lse = tail[0:1] + tail[1:2] + tail[2:3]
                before = own_lse[h, 0:1, :]
                top = jnp.maximum(before, lse)
                keep, add = jnp.exp(before - top), jnp.exp(lse - top)
                own_o[h] = own_o[h] * keep + orecv[d - 1, h, :HD, :].astype(F32) * add
                own_lse[h, 0:1, :] = top
                own_lse[h, 1:2, :] = own_lse[h, 1:2, :] * keep + add

        so[:, hcols(h)] = (own_o[h] * (1.0 / own_lse[h, 1:2, :])).T.astype(BF16)

    self_store = pltpu.make_async_copy(so, self_out, out_sem.at[4])
    self_store.start()

    @pl.when(has_prev)
    def _():
        edge_query().wait_send()

    @pl.when(has_next)
    def _():
        edge_grad().wait_send()

    for dl, dh in plane_offsets:
        sq1_copy(dl, dh).wait_send()
    for d in range(1, groups):
        sq2_copy(d).wait_send()

    @pl.loop(0, heads)
    def _(h):
        for d in range(1, group):
            kv_copy(d, h, 0, lo).wait_send()
            kv_copy(d, h, 1, lo).wait_send()

        @pl.loop(1, groups)
        def _(d):
            @pl.when(hi >= d)
            def _():
                q_copy(d, h).wait_send()

            @pl.when(hi + d < groups)
            def _():
                o_copy(d, h).wait_send()

    cross_store.wait()
    query_store.wait()
    keys_store.wait()
    values_store.wait()
    self_store.wait()


def body(nctx, nhead, q_self, k_self, v_self, q_cross, n_keys, n_values, d_cross):
    rows, cols = q_self.shape
    nrows = n_keys.shape[0]
    heads = cols // HD
    group = 4 if nctx % 4 == 0 else nctx
    groups = nctx // group
    far = max(groups - 1, 1)
    dma = pltpu.SemaphoreType.DMA
    spec = pl.BlockSpec(memory_space=pl.ANY)
    small = jax.ShapeDtypeStruct((rows, cols), BF16)
    large = jax.ShapeDtypeStruct((nrows, cols), BF16)
    return pl.pallas_call(
        functools.partial(kernel, nctx, nhead, group, 2.0 * nrows * cols * nctx * nhead),
        out_shape=(small, small, small, large, large),
        in_specs=[spec] * 7,
        out_specs=(spec,) * 5,
        scratch_shapes=[
            pltpu.VMEM((group, rows, cols), BF16),
            pltpu.VMEM((group, rows, cols), BF16),
            pltpu.VMEM((groups, rows, cols), BF16),
            pltpu.VMEM((far, heads, HD + TAIL, rows), BF16),
            pltpu.VMEM((far, heads, HD + TAIL, rows), BF16),
            pltpu.VMEM((heads, HD, rows), F32),
            pltpu.VMEM((heads, 8, rows), F32),
            pltpu.VMEM((rows + SPAN, cols), BF16),
            pltpu.VMEM((nrows, cols), BF16),
            pltpu.VMEM((nrows, cols), BF16),
            pltpu.VMEM((rows, cols), BF16),
            pltpu.VMEM((rows, cols), BF16),
            pltpu.VMEM((rows + SPAN, cols), BF16),
            pltpu.VMEM((rows, cols), BF16),
            pltpu.VMEM((rows, cols), BF16),
            pltpu.VMEM((nrows, cols), F32),
            pltpu.VMEM((nrows, cols), F32),
            pltpu.VMEM((nrows, cols), BF16),
            pltpu.VMEM((nrows, cols), BF16),
            pltpu.VMEM((rows, cols), BF16),
            pltpu.VMEM((group * nhead, 8, HD), F32),
            pltpu.VMEM((groups, 8, HD), F32),
            dma((7,)),
            dma((5,)),
            dma((group - 1, heads, 2)),
            dma((group - 1, heads, 2)),
            dma((far, heads)),
            dma((far, heads)),
            dma((far, heads)),
            dma((far, heads)),
            dma((2,)),
            dma((2,)),
            dma((group * nhead,)),
            dma((group * nhead,)),
            dma((groups,)),
            dma((groups,)),
        ],
        compiler_params=pltpu.CompilerParams(
            collective_id=0, has_side_effects=True, vmem_limit_bytes=40 * 1024 * 1024
        ),
        cost_estimate=pl.CostEstimate(flops=10**9, bytes_accessed=4 * 10**6, transcendentals=10**6),
    )(q_self, k_self, v_self, q_cross, n_keys, n_values, d_cross)


def solution(mesh):
    spec = P("ctx", "head")
    return jax.shard_map(
        functools.partial(body, mesh.shape["ctx"], mesh.shape["head"]),
        mesh=mesh, in_specs=(spec,) * 7, out_specs=(spec,) * 5, check_vma=False,
    )
```

```python
import functools
import math

import jax
import jax.numpy as jnp
from jax import lax
from jax.experimental import pallas as pl
from jax.experimental.pallas import tpu as pltpu
from jax.sharding import PartitionSpec as P

HD = 128
SPAN = 64
LAG = SPAN - 1
TAIL = 16
F32 = jnp.float32
BF16 = jnp.bfloat16
NEG = -1e30


def dot(a, b, dims):
    return lax.dot_general(a, b, (dims, ((), ())), preferred_element_type=F32)


def kernel(
    nctx, nhead, group, total_elements,
    q_self, k_self, v_self, q_cross, n_keys, n_values, d_cross,
    self_out, cross_out, d_query, d_keys, d_values,
    kbuf, vbuf, qbuf, osend, orecv, own_o, own_lse,
    qc, nk, nv, dc, shifted, gsrc, cross, dq, gk, gv, dkb, dvb, so,
    sq1, sq2,
    load_sem, out_sem, kv_s, kv_r, q_s, q_r, o_s, o_r, edge_s, edge_r,
    sq1_s, sq1_r, sq2_s, sq2_r,
):
    groups = nctx // group
    rows, cols = q_self.shape
    heads = cols // HD
    nrows = n_keys.shape[0]
    scale = 1.0 / math.sqrt(HD)
    me = lax.axis_index("ctx")
    my_head = lax.axis_index("head")
    hi, lo = me // group, lax.rem(me, group)
    has_next = me < nctx - 1
    has_prev = me > 0

    def hcols(h):
        return pl.ds(pl.multiple_of(h * HD, HD), HD)

    loads = [
        pltpu.make_async_copy(q_cross, qc.at[pl.ds(0, rows)], load_sem.at[0]),
        pltpu.make_async_copy(n_keys, nk, load_sem.at[1]),
        pltpu.make_async_copy(n_values, nv, load_sem.at[2]),
        pltpu.make_async_copy(d_cross, dc, load_sem.at[3]),
        pltpu.make_async_copy(k_self, kbuf.at[lo], load_sem.at[4]),
        pltpu.make_async_copy(v_self, vbuf.at[lo], load_sem.at[5]),
        pltpu.make_async_copy(q_self, qbuf.at[0], load_sem.at[6]),
    ]
    for copy in loads:
        copy.start()

    barrier = pltpu.get_barrier_semaphore()

    def greet(ctx, head):
        pl.semaphore_signal(
            barrier, inc=1, device_id=(ctx, head), device_id_type=pl.DeviceIdType.MESH
        )

    def plane_peer(dl, dh):
        return hi * group + lax.rem(lo + dl, group), lax.rem(my_head + dh, nhead)

    plane_offsets = [(a, b) for a in range(group) for b in range(nhead) if a or b]
    for dl, dh in plane_offsets:
        greet(*plane_peer(dl, dh))
    for d in range(1, groups):
        greet(lax.rem(hi + d, groups) * group + lo, my_head)
    edge_up = jnp.logical_and(lo == group - 1, has_next)
    edge_down = jnp.logical_and(lo == 0, has_prev)

    @pl.when(edge_up)
    def _():
        greet(me + 1, my_head)

    @pl.when(edge_down)
    def _():
        greet(me - 1, my_head)

    pl.semaphore_wait(
        barrier,
        len(plane_offsets) + groups - 1
        + edge_up.astype(jnp.int32) + edge_down.astype(jnp.int32),
    )

    def remote(src, dst, send, recv, ctx, head=None):
        return pltpu.make_async_remote_copy(
            src_ref=src, dst_ref=dst, send_sem=send, recv_sem=recv,
            device_id=(ctx, my_head if head is None else head),
            device_id_type=pl.DeviceIdType.MESH,
        )

    def edge_query():
        return remote(
            q_cross.at[pl.ds(0, SPAN)], qc.at[pl.ds(rows, SPAN)],
            edge_s.at[0], edge_r.at[0], jnp.maximum(me - 1, 0),
        )

    def edge_grad():
        return remote(
            gsrc.at[pl.ds(rows, SPAN)], gsrc.at[pl.ds(0, SPAN)],
            edge_s.at[1], edge_r.at[1], jnp.minimum(me + 1, nctx - 1),
        )

    @pl.when(has_prev)
    def _():
        edge_query().start()

    def kv_copy(d, h, which, slot):
        src, buf = (k_self, kbuf) if which == 0 else (v_self, vbuf)
        return remote(
            src.at[:, hcols(h)], buf.at[slot, :, hcols(h)],
            kv_s.at[d - 1, h, which], kv_r.at[d - 1, h, which],
            hi * group + lax.rem(lo + d, group),
        )

    def q_copy(d, h):
        return remote(
            q_self.at[:, hcols(h)], qbuf.at[d, :, hcols(h)],
            q_s.at[d - 1, h], q_r.at[d - 1, h],
            jnp.maximum(hi - d, 0) * group + lo,
        )

    def o_copy(d, h):
        return remote(
            osend.at[d - 1, h], orecv.at[d - 1, h],
            o_s.at[d - 1, h], o_r.at[d - 1, h],
            jnp.minimum(hi + d, groups - 1) * group + lo,
        )

    @pl.loop(0, heads)
    def _(h):
        for d in range(1, group):
            kv_copy(d, h, 0, lo).start()
            kv_copy(d, h, 1, lo).start()

        @pl.loop(1, groups)
        def _(d):
            @pl.when(hi >= d)
            def _():
                q_copy(d, h).start()

    for copy in loads[:4]:
        copy.wait()

    @pl.when(has_next)
    def _():
        edge_query().wait_recv()

    @pl.when(jnp.logical_not(has_next))
    def _():
        qc[rows:, :] = jnp.zeros((SPAN, cols), BF16)

    row_id = lax.broadcasted_iota(jnp.int32, (rows, rows + SPAN), 0)
    col_id = lax.broadcasted_iota(jnp.int32, (rows, rows + SPAN), 1)
    pick = jnp.where(col_id == row_id + LAG, 1.0, 0.0).astype(BF16)
    shifted[...] = dot(pick, qc[...], ((1,), (0,))).astype(BF16)

    per_span = nrows // (rows // SPAN)
    neighbour = lax.broadcasted_iota(jnp.int32, (nrows, rows), 0)
    query = lax.broadcasted_iota(jnp.int32, (nrows, rows), 1)
    same_span = (neighbour // per_span) == (query // SPAN)

    def cross_head(h, squares):
        c = hcols(h)
        keys, values = nk[:, c], nv[:, c]
        queries, grads = shifted[:, c], dc[:, c]
        st = dot(keys, queries, ((1,), (1,))) * scale
        st = jnp.where(same_span, st, NEG)
        weights = jnp.exp(st - jnp.max(st, axis=0, keepdims=True))
        probs = weights * (1.0 / jnp.sum(weights, axis=0, keepdims=True))
        low = probs.astype(BF16)
        cross[:, c] = dot(low, values, ((0,), (0,))).astype(BF16)
        grad_probs = dot(values, grads, ((1,), (1,)))
        centre = jnp.sum(grad_probs * probs, axis=0, keepdims=True)
        grad_scores = (probs * (grad_probs - centre) * scale).astype(BF16)
        gsrc[SPAN:, c] = dot(grad_scores, keys, ((0,), (0,))).astype(BF16)
        grad_keys = dot(grad_scores, queries, ((1,), (0,)))
        gk[:, c] = grad_keys
        grad_values = dot(low, grads, ((1,), (0,)))
        gv[:, c] = grad_values
        return squares + jnp.sum(
            grad_keys * grad_keys + grad_values * grad_values, axis=0, keepdims=True
        )

    squares = lax.fori_loop(0, heads, cross_head, jnp.zeros((1, HD), F32))
    sq1[0] = jnp.broadcast_to(squares, (8, HD))

    def sq1_copy(dl, dh):
        slot = dl * nhead + dh
        ctx, head = plane_peer(dl, dh)
        return remote(
            sq1.at[0], sq1.at[slot], sq1_s.at[slot], sq1_r.at[slot], ctx, head
        )

    def sq2_copy(d):
        return remote(
            sq2.at[0], sq2.at[d], sq2_s.at[d], sq2_r.at[d],
            lax.rem(hi + d, groups) * group + lo,
        )

    for dl, dh in plane_offsets:
        sq1_copy(dl, dh).start()

    @pl.when(has_next)
    def _():
        edge_grad().start()

    cross_store = pltpu.make_async_copy(cross, cross_out, out_sem.at[0])
    cross_store.start()

    for copy in loads[4:]:
        copy.wait()

    def attend(st, values):
        largest = jnp.max(st, axis=0, keepdims=True)
        weights = jnp.exp(st - largest)
        total = jnp.sum(weights, axis=0, keepdims=True)
        mixed = dot(values, weights.astype(BF16), ((0,), (0,)))
        return mixed * (1.0 / total), largest + jnp.log(total)

    key_id = lax.broadcasted_iota(jnp.int32, (group * rows, rows), 0)
    query_id = lax.broadcasted_iota(jnp.int32, (group * rows, rows), 1)
    tail_id = lax.broadcasted_iota(jnp.int32, (TAIL, HD), 0)

    @pl.loop(0, heads)
    def _(h):
        c = hcols(h)
        for d in range(1, group):
            slot = lax.rem(lo + group - d, group)
            kv_copy(d, h, 0, slot).wait_recv()
            kv_copy(d, h, 1, slot).wait_recv()

        @pl.loop(1, groups)
        def _(step):
            d = groups - step

            @pl.when(hi + d < groups)
            def _():
                q_copy(d, h).wait_recv()
                keys = kbuf[:, :, c].reshape(group * rows, HD)
                values = vbuf[:, :, c].reshape(group * rows, HD)
                mixed, lse = attend(dot(keys, qbuf[d, :, c], ((1,), (1,))) * scale, values)
                osend[d - 1, h, :HD, :] = mixed.astype(BF16)
                high = lse.astype(BF16).astype(F32)
                rest = lse - high
                middle = rest.astype(BF16).astype(F32)
                tail = jnp.where(tail_id == 0, high, jnp.where(tail_id == 1, middle, rest - middle))
                osend[d - 1, h, HD:, :] = tail.astype(BF16)
                o_copy(d, h).start()

        keys = kbuf[:, :, c].reshape(group * rows, HD)
        values = vbuf[:, :, c].reshape(group * rows, HD)
        st = dot(keys, qbuf[0, :, c], ((1,), (1,))) * scale
        st = jnp.where(key_id <= query_id + lo * rows, st, NEG)
        mixed, lse = attend(st, values)
        own_o[h] = mixed
        own_lse[h] = jnp.broadcast_to(lse, (8, HD))

    for dl, dh in plane_offsets:
        sq1_copy(dl, dh).wait_recv()
    sq2[0] = jnp.sum(sq1[...], axis=0)
    for d in range(1, groups):
        sq2_copy(d).start()

    @pl.when(has_prev)
    def _():
        edge_grad().wait_recv()

    @pl.when(jnp.logical_not(has_prev))
    def _():
        gsrc[:SPAN, :] = jnp.zeros((SPAN, cols), BF16)

    back = jnp.where(col_id == row_id + 1, 1.0, 0.0).astype(BF16)
    dq[...] = dot(back, gsrc[...], ((1,), (0,))).astype(BF16)
    query_store = pltpu.make_async_copy(dq, d_query, out_sem.at[1])
    query_store.start()

    for d in range(1, groups):
        sq2_copy(d).wait_recv()
    overall = jnp.sum(jnp.sum(sq2[...], axis=0)[0:1, :], axis=1, keepdims=True)
    factor = lax.rsqrt(overall / total_elements + 1e-06)
    dkb[...] = (gk[...] * factor).astype(BF16)
    keys_store = pltpu.make_async_copy(dkb, d_keys, out_sem.at[2])
    keys_store.start()
    dvb[...] = (gv[...] * factor).astype(BF16)
    values_store = pltpu.make_async_copy(dvb, d_values, out_sem.at[3])
    values_store.start()

    @pl.loop(0, heads)
    def _(h):
        own_lse[h, 1:2, :] = jnp.ones((1, HD), F32)

        @pl.loop(1, groups)
        def _(d):
            @pl.when(hi >= d)
            def _():
                o_copy(d, h).wait_recv()
                tail = orecv[d - 1, h, HD:, :].astype(F32)
                lse = tail[0:1] + tail[1:2] + tail[2:3]
                before = own_lse[h, 0:1, :]
                top = jnp.maximum(before, lse)
                keep, add = jnp.exp(before - top), jnp.exp(lse - top)
                own_o[h] = own_o[h] * keep + orecv[d - 1, h, :HD, :].astype(F32) * add
                own_lse[h, 0:1, :] = top
                own_lse[h, 1:2, :] = own_lse[h, 1:2, :] * keep + add

        so[:, hcols(h)] = (own_o[h] * (1.0 / own_lse[h, 1:2, :])).T.astype(BF16)

    self_store = pltpu.make_async_copy(so, self_out, out_sem.at[4])
    self_store.start()

    @pl.when(has_prev)
    def _():
        edge_query().wait_send()

    @pl.when(has_next)
    def _():
        edge_grad().wait_send()

    for dl, dh in plane_offsets:
        sq1_copy(dl, dh).wait_send()
    for d in range(1, groups):
        sq2_copy(d).wait_send()

    @pl.loop(0, heads)
    def _(h):
        for d in range(1, group):
            kv_copy(d, h, 0, lo).wait_send()
            kv_copy(d, h, 1, lo).wait_send()

        @pl.loop(1, groups)
        def _(d):
            @pl.when(hi >= d)
            def _():
                q_copy(d, h).wait_send()

            @pl.when(hi + d < groups)
            def _():
                o_copy(d, h).wait_send()

    cross_store.wait()
    query_store.wait()
    keys_store.wait()
    values_store.wait()
    self_store.wait()


def write_out(*refs):
    sources, targets, held = refs[:5], refs[5:10], refs[10:15]
    in_sem, out_sem = refs[15], refs[16]
    order = (3, 4, 0, 1, 2)
    fetch = [pltpu.make_async_copy(sources[i], held[i], in_sem.at[i]) for i in range(5)]
    store = [pltpu.make_async_copy(held[i], targets[i], out_sem.at[i]) for i in range(5)]
    for i in order:
        fetch[i].start()
    for i in order:
        fetch[i].wait()
        store[i].start()
    for i in order:
        store[i].wait()


def body(nctx, nhead, q_self, k_self, v_self, q_cross, n_keys, n_values, d_cross):
    rows, cols = q_self.shape
    nrows = n_keys.shape[0]
    heads = cols // HD
    group = 4 if nctx % 4 == 0 else nctx
    groups = nctx // group
    far = max(groups - 1, 1)
    dma = pltpu.SemaphoreType.DMA
    spec = pl.BlockSpec(memory_space=pl.ANY)
    small = jax.ShapeDtypeStruct((rows, cols), BF16)
    large = jax.ShapeDtypeStruct((nrows, cols), BF16)
    results = pl.pallas_call(
        functools.partial(kernel, nctx, nhead, group, 2.0 * nrows * cols * nctx * nhead),
        out_shape=(small, small, small, large, large),
        in_specs=[spec] * 7,
        out_specs=(spec,) * 5,
        scratch_shapes=[
            pltpu.VMEM((group, rows, cols), BF16),
            pltpu.VMEM((group, rows, cols), BF16),
            pltpu.VMEM((groups, rows, cols), BF16),
            pltpu.VMEM((far, heads, HD + TAIL, rows), BF16),
            pltpu.VMEM((far, heads, HD + TAIL, rows), BF16),
            pltpu.VMEM((heads, HD, rows), F32),
            pltpu.VMEM((heads, 8, rows), F32),
            pltpu.VMEM((rows + SPAN, cols), BF16),
            pltpu.VMEM((nrows, cols), BF16),
            pltpu.VMEM((nrows, cols), BF16),
            pltpu.VMEM((rows, cols), BF16),
            pltpu.VMEM((rows, cols), BF16),
            pltpu.VMEM((rows + SPAN, cols), BF16),
            pltpu.VMEM((rows, cols), BF16),
            pltpu.VMEM((rows, cols), BF16),
            pltpu.VMEM((nrows, cols), F32),
            pltpu.VMEM((nrows, cols), F32),
            pltpu.VMEM((nrows, cols), BF16),
            pltpu.VMEM((nrows, cols), BF16),
            pltpu.VMEM((rows, cols), BF16),
            pltpu.VMEM((group * nhead, 8, HD), F32),
            pltpu.VMEM((groups, 8, HD), F32),
            dma((7,)),
            dma((5,)),
            dma((group - 1, heads, 2)),
            dma((group - 1, heads, 2)),
            dma((far, heads)),
            dma((far, heads)),
            dma((far, heads)),
            dma((far, heads)),
            dma((2,)),
            dma((2,)),
            dma((group * nhead,)),
            dma((group * nhead,)),
            dma((groups,)),
            dma((groups,)),
        ],
        compiler_params=pltpu.CompilerParams(
            collective_id=0, has_side_effects=True, vmem_limit_bytes=63 * 1024 * 1024
        ),
        cost_estimate=pl.CostEstimate(flops=10**9, bytes_accessed=4 * 10**6, transcendentals=10**6),
    )(q_self, k_self, v_self, q_cross, n_keys, n_values, d_cross)
    return pl.pallas_call(
        write_out,
        out_shape=(small, small, small, large, large),
        in_specs=[spec] * 5,
        out_specs=(spec,) * 5,
        scratch_shapes=[pltpu.VMEM((rows, cols), BF16)] * 3
        + [pltpu.VMEM((nrows, cols), BF16)] * 2
        + [dma((5,)), dma((5,))],
        compiler_params=pltpu.CompilerParams(vmem_limit_bytes=63 * 1024 * 1024),
    )(*results)


def solution(mesh):
    spec = P("ctx", "head")
    return jax.shard_map(
        functools.partial(body, mesh.shape["ctx"], mesh.shape["head"]),
        mesh=mesh, in_specs=(spec,) * 7, out_specs=(spec,) * 5, check_vma=False,
    )
```
